32 devices in a mesh: sec: 16 (over z, y, core), narrow: 2 (over x).
Axes of the slice: x: 2, y: 2, z: 4, core: 2. Of those that a mesh axis runs over, the one named last changes fastest.
Arguments:
- tokens: bfloat16 [2048, 2048], P('sec'), may hold values from -8 to 8
- attn_gain: float32 [2048], replicated, may hold values from 0.5 to 1.5
- w_query: bfloat16 [2048, 4096], P(None, 'narrow'), may hold values from -0.125 to 0.125
- w_key: bfloat16 [2048, 512], P(None, 'narrow'), may hold values from -0.125 to 0.125
- w_value: bfloat16 [2048, 512], P(None, 'narrow'), may hold values from -0.125 to 0.125
- query_gain: float32 [128], replicated, may hold values from 0.6 to 6
- key_gain: float32 [128], replicated, may hold values from 0.6 to 6
- w_out: bfloat16 [4096, 2048], P('narrow'), may hold values from -0.09375 to 0.09375
- moe_gain: float32 [2048], replicated, may hold values from 0.5 to 1.5
- expert_ids: int32 [2048, 8], P('sec'), may hold values from 0 to 63, all different within a row; in each aligned block of 64 rows (0 to 63, 64 to 127, ...) at most 20 rows name the same one
- expert_weights: float32 [2048, 8], P('sec'), may hold values from 0.05 to 1
- w_gate: bfloat16 [64, 2048, 768], P('sec', None, 'narrow'), may hold values from -0.125 to 0.125
- w_up: bfloat16 [64, 2048, 768], P('sec', None, 'narrow'), may hold values from -0.125 to 0.125
- w_down: bfloat16 [64, 768, 2048], P('sec', 'narrow'), may hold values from -0.21875 to 0.21875
Outputs:
- layer_out: bfloat16 [2048, 2048], P(('sec', 'narrow'))
The draws below stay inside these ranges and needn't reach their ends.
Inputs may be any that keep to these rules, and one draw needn't show every extreme that they name: `expert_ids`: each row names 8 different experts. In each aligned block of 64 rows no expert is named by more than 20 rows, a bound that some block reaches.
All inputs are finite; a program needn't handle non-finite values.
Results may differ from the reference program's by a relative error of at most 0.009.
Values may be sent and summed in bfloat16 or wider, within the bound.
A program may use at most 128 MiB of HBM per device.

```python
import math
import jax
import jax.numpy as jnp
import numpy as np
from jax import lax

D = 2048
HEADS = 32
KV_HEADS = 4
HEAD = 128
FE = 768
TOPK = 8
EXPERTS = 64
TOKENS = 2048
ROWS_N = 64
CAP = 20
N_NARROW = 2


def draw_tokens(key, part):
    noise_key = jax.random.fold_in(key, 0)
    noise = jax.random.normal(noise_key, (TOKENS, D), jnp.float32)
    drawn = noise
    return jnp.clip(drawn, -8.0, 8.0).astype(jnp.bfloat16)


def gain_values(key, salt):
    inner = jax.random.fold_in(key, salt)
    return jax.random.uniform(inner, (HEAD,), jnp.float32, 0.6, 1.6)


def draw_query_gain(key, part):
    return gain_values(key, 11)


def draw_key_gain(key, part):
    return gain_values(key, 23)


def shard_levels(stream_key, shape, shards, smallest, largest):
    level = 1.0
    for axis_at, shards_of in shards:
        steps = jax.random.uniform(jax.random.fold_in(jax.random.fold_in(stream_key, 6), axis_at), (shards_of,), jnp.float32, smallest / len(shards), largest / len(shards))
        level = level * jnp.repeat(jnp.exp(steps), shape[axis_at] // shards_of).reshape((-1,) + (1,) * (len(shape) - 1 - axis_at))
    return level


def deal_out(rng, own, number, rows, amount, top, limit, lean):
    ranking = jax.random.permutation(rng, amount)
    heavy_load, ordinary = portions_of(amount, rows * top, limit, lean, True), portions_of(amount, rows * top, limit, lean, False)
    places = jnp.arange(amount)

    def named(tallies, offset_by):
        used = int((tallies > 0).sum())
        fixed = max(1, used // 4)
        moved = fixed + (places - fixed + offset_by * (used - fixed)) % max(1, amount - fixed)
        return jnp.zeros((amount,), jnp.int32).at[ranking[jnp.where(places < fixed, places, moved)]].set(jnp.asarray(tallies, jnp.int32))

    tallies = jnp.where(number % 4 == 0, named(heavy_load, number // 4), named(ordinary, number - number // 4 - 1))
    mixed = jax.random.permutation(jax.random.fold_in(own, 3), amount)
    donor, receiver = mixed[0:amount // 2 * 2:2], mixed[1:amount // 2 * 2:2]
    margin = jnp.minimum(tallies[donor] - 1, limit - tallies[receiver]) // 2
    margin = jnp.where((donor == ranking[0]) | (receiver == ranking[0]) | (tallies[receiver] == 0), 0, jnp.maximum(margin, 0))
    moved = jax.random.randint(jax.random.fold_in(own, 4), (amount // 2,), 0, 1 << 20) % (margin + 1)
    tallies = tallies.at[donor].add(-moved).at[receiver].add(moved)
    items = jnp.searchsorted(jnp.cumsum(tallies), jnp.arange(rows * top), side="right").astype(jnp.int32)
    listing = items.reshape(top, rows).T
    listing = listing[jax.random.permutation(jax.random.fold_in(own, 1), rows)]
    offset_by = jax.random.randint(jax.random.fold_in(own, 2), (rows, 1), 0, top)
    return jnp.take_along_axis(listing, (jnp.arange(top)[None, :] + offset_by) % top, axis=1)


def portions_of(number_of, total, reach, slope, full):
    portions = [(1 << 20) // math.isqrt(grade ** slope) + 1 for grade in range(1, number_of + 1)]
    largest = reach if full else min(reach, max(-(-total // number_of), total * portions[0] // sum(portions)))
    least = 1 if total - largest >= number_of - 1 else 0
    counts, rest = [largest] + [least] * (number_of - 1), total - largest - least * (number_of - 1)
    while rest > 0:
        movable = [i for i in range(1, number_of) if counts[i] < largest] or [i for i in range(1, number_of) if counts[i] < reach]
        mass, left = sum([portions[i] for i in movable]), rest
        for i in movable:
            extra = min(reach - counts[i], max(1, left * portions[i] // mass), rest)
            counts[i] = counts[i] + extra
            rest = rest - extra
    return np.array(counts)


def normal_values(rng, extent, spread, most, cuts=(), held_as=jnp.bfloat16):
    values = jax.random.normal(rng, extent, jnp.float32) * spread
    if len(cuts) > 0:
        values = shard_levels(rng, extent, cuts, -0.22, 0.18) * values
    return jnp.clip(values, min=-most, max=most).astype(held_as)


def setup_inputs(seed: int = 0) -> dict:
    arg_keys = jax.random.split(jax.random.key(seed), 15)
    tokens = draw_tokens(jax.random.fold_in(arg_keys[14], 71), 0)
    attn_gain = jnp.clip(1.0 + 0.1 * jax.random.normal(arg_keys[1], (D,), jnp.float32), 0.5, 1.5)
    w_query = normal_values(arg_keys[2], (D, HEADS * HEAD), D ** -0.5, 0.125, ((1, 2),))
    w_key = normal_values(arg_keys[3], (D, KV_HEADS * HEAD), D ** -0.5, 0.125, ((1, 2),))
    w_value = normal_values(arg_keys[4], (D, KV_HEADS * HEAD), D ** -0.5, 0.125, ((1, 2),))
    query_gain = draw_query_gain(jax.random.fold_in(arg_keys[14], 71), 0)
    key_gain = draw_key_gain(jax.random.fold_in(arg_keys[14], 71), 0)
    w_out = normal_values(arg_keys[7], (HEADS * HEAD, D), (HEADS * HEAD) ** -0.5, 0.09375, ((0, 2),))
    moe_gain = jnp.clip(1.0 + 0.1 * jax.random.normal(arg_keys[8], (D,), jnp.float32), 0.5, 1.5)
    expert_ids_keys = jax.random.split(jax.random.fold_in(arg_keys[9], 1), TOKENS // ROWS_N)
    expert_ids_turns = jax.random.permutation(jax.random.fold_in(arg_keys[9], 3), TOKENS // ROWS_N)
    expert_ids = jax.vmap(lambda own, number: deal_out(jax.random.fold_in(arg_keys[9], 2), own, number, ROWS_N, EXPERTS, TOPK, CAP, 2))(expert_ids_keys, expert_ids_turns).reshape((TOKENS, TOPK))
    expert_weights = jnp.clip(jnp.exp(math.log(1.0) - 2.9957323 * jax.random.uniform(arg_keys[10], (TOKENS, TOPK), jnp.float32) ** shard_levels(arg_keys[10], (TOKENS, TOPK), ((0, 16),), -0.2, 0.2)), 0.05, 1.0)
    w_gate = normal_values(arg_keys[11], (EXPERTS, D, FE), D ** -0.5, 0.125, ((0, 16), (2, 2)))
    w_up = normal_values(arg_keys[12], (EXPERTS, D, FE), D ** -0.5, 0.125, ((0, 16), (2, 2)))
    w_down = normal_values(arg_keys[13], (EXPERTS, FE, D), FE ** -0.5, 0.21875, ((0, 16), (1, 2)))
    return {"tokens": tokens, "attn_gain": attn_gain, "w_query": w_query, "w_key": w_key, "w_value": w_value, "query_gain": query_gain, "key_gain": key_gain, "w_out": w_out, "moe_gain": moe_gain, "expert_ids": expert_ids, "expert_weights": expert_weights, "w_gate": w_gate, "w_up": w_up, "w_down": w_down}


norm_eps = 1e-06

def rms_norm(inputs, gain):
    widened = inputs.astype(jnp.float32)
    return widened * lax.rsqrt(lax.optimization_barrier(jnp.mean(widened * widened, axis=-1, keepdims=True)) + norm_eps) * gain

def rotate(inputs, positions):
    half_size = inputs.shape[-1] // 2
    inverse = jnp.exp(-jnp.log(1000000.0) * jnp.arange(half_size, dtype=jnp.float32) * 2.0 / inputs.shape[-1])
    angles = positions.astype(jnp.float32)[:, None] * inverse[None, :]
    cosine = jnp.cos(angles)[:, None, :]
    sine = jnp.sin(angles)[:, None, :]
    leading = inputs[..., :half_size]
    trailing = inputs[..., half_size:]
    return jnp.concatenate([leading * cosine - trailing * sine, trailing * cosine + leading * sine], axis=-1)

def reference(tokens, attn_gain, w_query, w_key, w_value, query_gain, key_gain, w_out, moe_gain, expert_ids, expert_weights, w_gate, w_up, w_down):
    length = tokens.shape[0]
    positions = jnp.arange(length, dtype=jnp.int32)
    normed = rms_norm(tokens, attn_gain).astype(jnp.bfloat16)
    query = jnp.dot(normed, w_query, preferred_element_type=jnp.float32).reshape(length, HEADS, HEAD)
    query = rotate(rms_norm(query, query_gain), positions).astype(jnp.bfloat16)
    keys = jnp.dot(normed, w_key, preferred_element_type=jnp.float32).reshape(length, HEAD, KV_HEADS)
    keys = jnp.transpose(keys, (0, 2, 1))
    keys = rotate(rms_norm(keys, key_gain), positions).astype(jnp.bfloat16)
    values = jnp.dot(normed, w_value, preferred_element_type=jnp.float32).astype(jnp.bfloat16).reshape(length, HEAD, KV_HEADS)
    values = jnp.transpose(values, (0, 2, 1))
    group_size = HEADS // KV_HEADS
    scale = 1.0 / math.sqrt(HEAD)
    allowed = positions[None, :] <= positions[:, None]
    key_heads = jnp.transpose(keys, (1, 0, 2))
    value_heads = jnp.transpose(values, (1, 0, 2))

    def one_head(inputs):
        query_head, number = inputs
        key_head = lax.dynamic_index_in_dim(key_heads, number // group_size, 0, keepdims=False)
        value_head = lax.dynamic_index_in_dim(value_heads, number // group_size, 0, keepdims=False)
        scores = jnp.dot(query_head, key_head.T, preferred_element_type=jnp.float32) * scale
        scores = jnp.where(allowed, scores, -1e+30)
        peak = lax.optimization_barrier(jnp.max(scores, axis=-1, keepdims=True))
        probs = jnp.where(allowed, jnp.exp(scores - peak), 0.0)
        summed = jnp.dot(probs.astype(jnp.bfloat16), value_head, preferred_element_type=jnp.float32)
        return (summed / lax.optimization_barrier(jnp.sum(probs, axis=-1, keepdims=True))).astype(jnp.bfloat16)
    attended = lax.map(one_head, (jnp.transpose(query, (1, 0, 2)), jnp.arange(HEADS, dtype=jnp.int32)))
    attended = jnp.transpose(attended, (1, 0, 2)).reshape(length, HEADS * HEAD)
    carried = (tokens.astype(jnp.float32) + jnp.dot(attended, w_out, preferred_element_type=jnp.float32)).astype(jnp.bfloat16)
    moe_in = rms_norm(carried, moe_gain).astype(jnp.bfloat16)
    gates = expert_weights / lax.optimization_barrier(jnp.sum(expert_weights, axis=-1, keepdims=True))
    blocks = length // ROWS_N
    flat_ids = expert_ids.reshape(blocks, ROWS_N * TOPK)
    onehot = (flat_ids[:, :, None] == jnp.arange(EXPERTS, dtype=jnp.int32)[None, None, :]).astype(jnp.int32)
    earlier = jnp.cumsum(onehot, axis=1) - onehot
    slots = lax.optimization_barrier(jnp.sum(earlier * onehot, axis=-1))
    per_expert = blocks * CAP
    places = flat_ids * per_expert + jnp.arange(blocks, dtype=jnp.int32)[:, None] * CAP + slots
    sources = jnp.arange(length * TOPK, dtype=jnp.int32) // TOPK
    table = jnp.full((EXPERTS * per_expert,), length, jnp.int32).at[places.reshape(-1)].set(sources)
    padded = jnp.concatenate([moe_in, jnp.zeros((1, D), jnp.bfloat16)], axis=0)
    routed = padded[table].reshape(EXPERTS, per_expert, D)
    group_width = FE // N_NARROW

    def one_expert(inputs):
        rows_in, gate_matrix, up_matrix, down_matrix = inputs
        gate_value = jnp.dot(rows_in, gate_matrix, preferred_element_type=jnp.float32)
        up_value = jnp.dot(rows_in, up_matrix, preferred_element_type=jnp.float32)
        active = (jax.nn.silu(gate_value) * up_value).astype(jnp.bfloat16)
        total = jnp.zeros((per_expert, D), jnp.float32)
        for group_index in range(N_NARROW):
            lower = group_index * group_width
            partial_term = jnp.dot(active[:, lower:lower + group_width], down_matrix[lower:lower + group_width], preferred_element_type=jnp.float32)
            rounded = lax.optimization_barrier(partial_term.astype(jnp.bfloat16))
            total = total + rounded.astype(jnp.float32)
        return total.astype(jnp.bfloat16)
    outputs = lax.map(one_expert, (routed, w_gate, w_up, w_down)).reshape(EXPERTS * per_expert, D)
    picked = outputs[places.reshape(-1)].reshape(length, TOPK, D)
    mixture = lax.optimization_barrier(jnp.sum(gates[:, :, None] * picked.astype(jnp.float32), axis=1))
    return (carried.astype(jnp.float32) + mixture).astype(jnp.bfloat16)
```

```python
import functools
import math

import jax
import jax.numpy as jnp
from jax import lax
from jax.experimental import pallas as pl
from jax.experimental.pallas import tpu as pltpu
from jax.sharding import PartitionSpec as P

D = 2048
HEADS = 32
KV_HEADS = 4
HEAD = 128
TOPK = 8


norm_eps = 1e-06


def rms_norm(inputs, gain):
    widened = inputs.astype(jnp.float32)
    return (
        widened * lax.rsqrt(jnp.mean(widened * widened, axis=-1, keepdims=True) + norm_eps) * gain
    )


def rotate(inputs, positions):
    half_size = inputs.shape[-1] // 2
    inverse = jnp.exp(
        -jnp.log(1000000.0) * jnp.arange(half_size, dtype=jnp.float32) * 2.0 / inputs.shape[-1]
    )
    angles = positions.astype(jnp.float32)[:, None] * inverse[None, :]
    cosine = jnp.cos(angles)[:, None, :]
    sine = jnp.sin(angles)[:, None, :]
    leading = inputs[..., :half_size]
    trailing = inputs[..., half_size:]
    return jnp.concatenate(
        [leading * cosine - trailing * sine, trailing * cosine + leading * sine], axis=-1
    )


VMEM_LIMIT = 60 * 1024 * 1024


def whole(shape):
    zeros = (0,) * len(shape)
    return pl.BlockSpec(shape, lambda *_: zeros, pipeline_mode=pl.Buffered(1))


def attention_kernel(width, local_rows, q_ref, k_ref, v_ref, o_ref):
    first = lax.axis_index("sec") * local_rows
    rows = q_ref.shape[0]
    q = q_ref[...]
    factor = math.log2(math.e) / math.sqrt(HEAD)
    positions = first + lax.rem(lax.broadcasted_iota(jnp.int32, (rows, width), 0), local_rows)
    columns = lax.broadcasted_iota(jnp.int32, (rows, width), 1)

    def advance(number, state):
        peak, total, accum = state
        start = pl.multiple_of(number * width, width)
        scores = lax.dot_general(
            q, k_ref[pl.ds(start, width), :], (((1,), (1,)), ((), ())),
            preferred_element_type=jnp.float32,
        ) * factor
        scores = jnp.where(columns + start <= positions, scores, -1e30)
        new_peak = jnp.maximum(peak, jnp.max(scores, axis=-1, keepdims=True))
        probs = jnp.exp2(scores - new_peak)
        shrink = jnp.exp2(peak - new_peak)
        total = total * shrink + jnp.sum(probs, axis=-1, keepdims=True)
        accum = accum * shrink + jnp.dot(
            probs.astype(jnp.bfloat16), v_ref[pl.ds(start, width), :],
            preferred_element_type=jnp.float32,
        )
        return new_peak, total, accum

    blocks = (first + local_rows - 1) // width + 1
    _, total, accum = lax.fori_loop(
        0,
        blocks,
        advance,
        (
            jnp.full((rows, 1), -1e30, jnp.float32),
            jnp.zeros((rows, 1), jnp.float32),
            jnp.zeros((rows, HEAD), jnp.float32),
        ),
    )
    o_ref[...] = (accum / total).astype(jnp.bfloat16)


def attention(query, keys_values, kv_here, per_key_head, local_rows):
    length = keys_values.shape[0]
    width = math.gcd(length, 512)
    together = math.gcd(per_key_head, 2)
    steps = per_key_head // together
    tall = together * local_rows
    return pl.pallas_call(
        functools.partial(attention_kernel, width, local_rows),
        grid=(kv_here, steps),
        in_specs=[
            pl.BlockSpec((tall, HEAD), lambda c, s: (c * steps + s, 0)),
            pl.BlockSpec((length, HEAD), lambda c, s: (0, c)),
            pl.BlockSpec((length, HEAD), lambda c, s: (0, kv_here + c)),
        ],
        out_specs=pl.BlockSpec((tall, HEAD), lambda c, s: (c * steps + s, 0)),
        out_shape=jax.ShapeDtypeStruct(query.shape, jnp.bfloat16),
        compiler_params=pltpu.CompilerParams(vmem_limit_bytes=VMEM_LIMIT),
    )(query, keys_values, keys_values)


def experts_kernel(x_ref, pick_ref, back_ref, weight_ref, gate_ref, up_ref, down_ref, o_ref, rows_ref, y_ref):
    step = pl.program_id(0)
    blocks, slots, block_rows = pick_ref.shape[1:]
    experts = y_ref.shape[0]
    for b in range(blocks):
        rows_ref[b * slots : (b + 1) * slots, :] = jnp.dot(
            pick_ref[0, b], x_ref[b * block_rows : (b + 1) * block_rows, :],
            preferred_element_type=jnp.float32,
        ).astype(jnp.bfloat16)
    rows = rows_ref[...]
    gate = jnp.dot(rows, gate_ref[0], preferred_element_type=jnp.float32)
    up = jnp.dot(rows, up_ref[0], preferred_element_type=jnp.float32)
    active = (gate / (1.0 + jnp.exp(-gate)) * up).astype(jnp.bfloat16)
    tile = math.gcd(o_ref.shape[1], 512)
    for c in range(0, o_ref.shape[1], tile):
        y_ref[step, :, c : c + tile] = (
            jnp.dot(active, down_ref[0, :, c : c + tile], preferred_element_type=jnp.float32)
            * weight_ref[0]
        ).astype(jnp.bfloat16)

    @pl.when(step == experts - 1)
    def _():
        for b in range(blocks):
            total = jnp.zeros((block_rows, o_ref.shape[1]), jnp.float32)
            for e in range(experts):
                total += jnp.dot(
                    back_ref[e, b], y_ref[e, b * slots : (b + 1) * slots, :],
                    preferred_element_type=jnp.float32,
                )
            o_ref[b * block_rows : (b + 1) * block_rows, :] = total.astype(jnp.bfloat16)


def experts_local(x, ids, gates, capacity, w_gate, w_up, w_down, first_expert):
    rows_all = x.shape[0]
    block_rows, slots = capacity
    experts = w_gate.shape[0]
    hidden = w_gate.shape[2]
    blocks = rows_all // block_rows
    mine = ids[:, :, None] == first_expert + jnp.arange(experts, dtype=jnp.int32)[None, None, :]
    hit = jnp.any(mine, axis=1)
    weight = jnp.sum(jnp.where(mine, gates[:, :, None], 0.0), axis=1)
    hit_blocks = hit.reshape(blocks, block_rows, experts).transpose(2, 0, 1)
    weight_blocks = weight.reshape(blocks, block_rows, experts).transpose(2, 0, 1)
    order = jnp.arange(block_rows, dtype=jnp.int32)
    before = (order[:, None] < order[None, :]).astype(jnp.bfloat16)
    rank = jnp.dot(
        hit_blocks.astype(jnp.bfloat16).reshape(experts * blocks, block_rows), before,
        preferred_element_type=jnp.float32,
    ).reshape(experts, blocks, block_rows).astype(jnp.int32)
    rank = jnp.where(hit_blocks, rank, -1)
    number = jnp.arange(slots, dtype=jnp.int32)
    taken = rank[:, :, None, :] == number[None, None, :, None]
    pick = taken.astype(jnp.bfloat16)
    back = (rank[:, :, :, None] == number[None, None, None, :]).astype(jnp.bfloat16)
    slot_weight = jnp.sum(
        jnp.where(taken, weight_blocks[:, :, None, :], 0.0), axis=-1
    ).reshape(experts, blocks * slots, 1)
    total = blocks * slots
    return pl.pallas_call(
        experts_kernel,
        grid=(experts,),
        in_specs=[
            whole(x.shape),
            pl.BlockSpec((1, blocks, slots, block_rows), lambda e: (e, 0, 0, 0)),
            whole(back.shape),
            pl.BlockSpec((1, total, 1), lambda e: (e, 0, 0)),
            pl.BlockSpec((1, D, hidden), lambda e: (e, 0, 0)),
            pl.BlockSpec((1, D, hidden), lambda e: (e, 0, 0)),
            pl.BlockSpec((1, hidden, D), lambda e: (e, 0, 0)),
        ],
        out_specs=whole(x.shape),
        out_shape=jax.ShapeDtypeStruct(x.shape, jnp.bfloat16),
        scratch_shapes=[
            pltpu.VMEM((total, D), jnp.bfloat16),
            pltpu.VMEM((experts, total, D), jnp.bfloat16),
        ],
        compiler_params=pltpu.CompilerParams(vmem_limit_bytes=VMEM_LIMIT),
    )(x, pick, back, slot_weight, w_gate, w_up, w_down)


def exchange(pieces_for, count, index, axis):
    own = pieces_for(index)
    held = jnp.zeros((count,) + own.shape, own.dtype)
    held = lax.dynamic_update_slice_in_dim(held, own[None], index, 0)
    for shift in range(1, count):
        target = lax.rem(index + shift, count)
        source = lax.rem(index + count - shift, count)
        piece = lax.ppermute(
            pieces_for(target), axis, [(i, (i + shift) % count) for i in range(count)]
        )
        held = lax.dynamic_update_slice_in_dim(held, piece[None], source, 0)
    return held


def on_device(
    tokens, attn_gain, w_query, w_key, w_value, query_gain, key_gain, w_out, moe_gain,
    expert_ids, expert_weights, w_gate, w_up, w_down,
):
    sec_count = lax.axis_size("sec")
    narrow_count = lax.axis_size("narrow")
    sec_index = lax.axis_index("sec")
    narrow_index = lax.axis_index("narrow")
    local_rows = tokens.shape[0]
    share_rows = local_rows // narrow_count
    expert_here = w_gate.shape[0]
    experts_all = expert_here * sec_count
    capacity = min(share_rows, max(2, 5 * share_rows * TOPK // (2 * experts_all)))
    heads_here = w_query.shape[1] // HEAD
    group_size = HEADS // KV_HEADS
    kv_here = max(1, heads_here // group_size)
    per_key_head = heads_here // kv_here
    part = HEAD // narrow_count
    positions = sec_index * local_rows + jnp.arange(local_rows, dtype=jnp.int32)
    normed = rms_norm(tokens, attn_gain).astype(jnp.bfloat16)

    columns = jnp.arange(w_key.shape[1], dtype=jnp.int32)
    sorted_at = columns % KV_HEADS * part + columns // KV_HEADS
    order = (sorted_at[:, None] == columns[None, :]).astype(jnp.bfloat16)
    both = jnp.concatenate(
        [
            jnp.dot(w, order, preferred_element_type=jnp.float32).astype(jnp.bfloat16)
            for w in (w_key, w_value)
        ],
        axis=1,
    )
    kv_part = jnp.dot(normed, both, preferred_element_type=jnp.float32)
    kv_part = kv_part.reshape(local_rows, 2, KV_HEADS * part)

    def for_peer(peer):
        start = peer * heads_here // group_size * part
        return lax.dynamic_slice_in_dim(kv_part, start, kv_here * part, 2)

    held = exchange(for_peer, narrow_count, narrow_index, "narrow")
    held = held.reshape(narrow_count, local_rows, 2, kv_here, part)
    held = jnp.transpose(held, (1, 2, 3, 0, 4)).reshape(local_rows, 2, kv_here, HEAD)
    keys = rotate(rms_norm(held[:, 0], key_gain), positions).astype(jnp.bfloat16)
    values = held[:, 1].astype(jnp.bfloat16)

    gates_own = expert_weights / jnp.sum(expert_weights, axis=-1, keepdims=True)
    keys_values = jnp.concatenate([keys, values], axis=1).reshape(local_rows, 2 * kv_here * HEAD)
    keys_values = lax.all_gather(keys_values, "sec", axis=0, tiled=True)
    routing = lax.all_gather(
        jnp.concatenate([expert_ids.astype(jnp.float32), gates_own], axis=1), "sec", axis=0,
        tiled=True,
    )
    ids = routing[:, :TOPK].astype(jnp.int32)
    gates = routing[:, TOPK:]

    query = jnp.dot(normed, w_query, preferred_element_type=jnp.float32).reshape(
        local_rows, heads_here, HEAD
    )
    query = rotate(rms_norm(query, query_gain), positions).astype(jnp.bfloat16)
    query = jnp.transpose(query, (1, 0, 2)).reshape(heads_here * local_rows, HEAD)
    attended = attention(query, keys_values, kv_here, per_key_head, local_rows)
    attended = jnp.transpose(
        attended.reshape(heads_here, local_rows, HEAD), (1, 0, 2)
    ).reshape(local_rows, heads_here * HEAD)

    own_offset = narrow_index * share_rows
    mixed = jnp.dot(attended, w_out, preferred_element_type=jnp.float32).astype(jnp.bfloat16)
    mixed = exchange(
        lambda peer: lax.dynamic_slice_in_dim(mixed, peer * share_rows, share_rows, 0),
        narrow_count, narrow_index, "narrow",
    )
    mixed = jnp.sum(mixed.astype(jnp.float32), axis=0)
    tokens_mine = lax.dynamic_slice_in_dim(tokens, own_offset, share_rows, 0)
    carried = (tokens_mine.astype(jnp.float32) + mixed).astype(jnp.bfloat16)
    moe_in = rms_norm(carried, moe_gain).astype(jnp.bfloat16)
    moe_all = lax.all_gather(moe_in, ("sec", "narrow"), axis=0, tiled=True)

    block_rows, slots = local_rows, narrow_count * capacity
    while slots % 16:
        block_rows, slots = 2 * block_rows, 2 * slots
    mixture = experts_local(
        moe_all, ids, gates, (block_rows, slots), w_gate, w_up, w_down, sec_index * expert_here
    )
    mixture = lax.psum_scatter(mixture, ("sec", "narrow"), scatter_dimension=0, tiled=True)
    return (carried.astype(jnp.float32) + mixture.astype(jnp.float32)).astype(jnp.bfloat16)


def solution(mesh):
    in_specs = (
        P("sec", None),
        P(),
        P(None, "narrow"),
        P(None, "narrow"),
        P(None, "narrow"),
        P(),
        P(),
        P("narrow", None),
        P(),
        P("sec", None),
        P("sec", None),
        P("sec", None, "narrow"),
        P("sec", None, "narrow"),
        P("sec", "narrow", None),
    )
    out_specs = P(("sec", "narrow"), None)
    return jax.shard_map(
        on_device, mesh=mesh, in_specs=in_specs, out_specs=out_specs, check_vma=False
    )
```

```python
import functools
import math

import jax
import jax.numpy as jnp
from jax import lax
from jax.experimental import pallas as pl
from jax.experimental.pallas import tpu as pltpu
from jax.sharding import PartitionSpec as P

D = 2048
HEADS = 32
KV_HEADS = 4
HEAD = 128
TOPK = 8


norm_eps = 1e-06


def rms_norm(inputs, gain):
    widened = inputs.astype(jnp.float32)
    return (
        widened * lax.rsqrt(jnp.mean(widened * widened, axis=-1, keepdims=True) + norm_eps) * gain
    )


def rotate(inputs, positions):
    half_size = inputs.shape[-1] // 2
    inverse = jnp.exp(
        -jnp.log(1000000.0) * jnp.arange(half_size, dtype=jnp.float32) * 2.0 / inputs.shape[-1]
    )
    angles = positions.astype(jnp.float32)[:, None] * inverse[None, :]
    cosine = jnp.cos(angles)[:, None, :]
    sine = jnp.sin(angles)[:, None, :]
    leading = inputs[..., :half_size]
    trailing = inputs[..., half_size:]
    return jnp.concatenate(
        [leading * cosine - trailing * sine, trailing * cosine + leading * sine], axis=-1
    )


VMEM_LIMIT = 60 * 1024 * 1024


def whole(shape):
    zeros = (0,) * len(shape)
    return pl.BlockSpec(shape, lambda *_: zeros, pipeline_mode=pl.Buffered(1))


def attention_kernel(width, local_rows, q_ref, k_ref, v_ref, o_ref):
    first = lax.axis_index("sec") * local_rows
    rows = q_ref.shape[0]
    q = q_ref[...]
    factor = math.log2(math.e) / math.sqrt(HEAD)
    positions = first + lax.rem(lax.broadcasted_iota(jnp.int32, (rows, width), 0), local_rows)
    columns = lax.broadcasted_iota(jnp.int32, (rows, width), 1)

    def advance(number, state):
        peak, total, accum = state
        start = pl.multiple_of(number * width, width)
        scores = lax.dot_general(
            q, k_ref[pl.ds(start, width), :], (((1,), (1,)), ((), ())),
            preferred_element_type=jnp.float32,
        ) * factor
        scores = jnp.where(columns + start <= positions, scores, -1e30)
        new_peak = jnp.maximum(peak, jnp.max(scores, axis=-1, keepdims=True))
        probs = jnp.exp2(scores - new_peak)
        shrink = jnp.exp2(peak - new_peak)
        total = total * shrink + jnp.sum(probs, axis=-1, keepdims=True)
        accum = accum * shrink + jnp.dot(
            probs.astype(jnp.bfloat16), v_ref[pl.ds(start, width), :],
            preferred_element_type=jnp.float32,
        )
        return new_peak, total, accum

    blocks = (first + local_rows - 1) // width + 1
    _, total, accum = lax.fori_loop(
        0,
        blocks,
        advance,
        (
            jnp.full((rows, 1), -1e30, jnp.float32),
            jnp.zeros((rows, 1), jnp.float32),
            jnp.zeros((rows, HEAD), jnp.float32),
        ),
    )
    o_ref[...] = (accum / total).astype(jnp.bfloat16)


def attention(query, keys_values, kv_here, per_key_head, local_rows):
    length = keys_values.shape[0]
    width = math.gcd(length, 512)
    together = math.gcd(per_key_head, 2)
    steps = per_key_head // together
    tall = together * local_rows
    return pl.pallas_call(
        functools.partial(attention_kernel, width, local_rows),
        grid=(kv_here, steps),
        in_specs=[
            pl.BlockSpec((tall, HEAD), lambda c, s: (c * steps + s, 0)),
            pl.BlockSpec((length, HEAD), lambda c, s: (0, c)),
            pl.BlockSpec((length, HEAD), lambda c, s: (0, kv_here + c)),
        ],
        out_specs=pl.BlockSpec((tall, HEAD), lambda c, s: (c * steps + s, 0)),
        out_shape=jax.ShapeDtypeStruct(query.shape, jnp.bfloat16),
        compiler_params=pltpu.CompilerParams(vmem_limit_bytes=VMEM_LIMIT),
    )(query, keys_values, keys_values)


def experts_kernel(x_ref, pick_ref, back_ref, weight_ref, gate_ref, up_ref, down_ref, o_ref, rows_ref, y_ref):
    step = pl.program_id(0)
    blocks, slots, block_rows = pick_ref.shape[1:]
    experts = y_ref.shape[0]
    for b in range(blocks):
        rows_ref[b * slots : (b + 1) * slots, :] = jnp.dot(
            pick_ref[0, b], x_ref[b * block_rows : (b + 1) * block_rows, :],
            preferred_element_type=jnp.float32,
        ).astype(jnp.bfloat16)
    rows = rows_ref[...]
    gate = jnp.dot(rows, gate_ref[0], preferred_element_type=jnp.float32)
    up = jnp.dot(rows, up_ref[0], preferred_element_type=jnp.float32)
    active = (gate / (1.0 + jnp.exp(-gate)) * up).astype(jnp.bfloat16)
    tile = math.gcd(o_ref.shape[1], 512)
    for c in range(0, o_ref.shape[1], tile):
        y_ref[step, :, c : c + tile] = (
            jnp.dot(active, down_ref[0, :, c : c + tile], preferred_element_type=jnp.float32)
            * weight_ref[0]
        ).astype(jnp.bfloat16)

    @pl.when(step == experts - 1)
    def _():
        for b in range(blocks):
            total = jnp.zeros((block_rows, o_ref.shape[1]), jnp.float32)
            for e in range(experts):
                total += jnp.dot(
                    back_ref[e, b], y_ref[e, b * slots : (b + 1) * slots, :],
                    preferred_element_type=jnp.float32,
                )
            o_ref[b * block_rows : (b + 1) * block_rows, :] = total.astype(jnp.bfloat16)


def experts_local(x, ids, gates, capacity, w_gate, w_up, w_down, first_expert):
    rows_all = x.shape[0]
    block_rows, slots = capacity
    experts = w_gate.shape[0]
    hidden = w_gate.shape[2]
    blocks = rows_all // block_rows
    mine = ids[:, :, None] == first_expert + jnp.arange(experts, dtype=jnp.int32)[None, None, :]
    hit = jnp.any(mine, axis=1)
    weight = jnp.sum(jnp.where(mine, gates[:, :, None], 0.0), axis=1)
    hit_blocks = hit.reshape(blocks, block_rows, experts).transpose(2, 0, 1)
    weight_blocks = weight.reshape(blocks, block_rows, experts).transpose(2, 0, 1)
    order = jnp.arange(block_rows, dtype=jnp.int32)
    before = (order[:, None] < order[None, :]).astype(jnp.bfloat16)
    rank = jnp.dot(
        hit_blocks.astype(jnp.bfloat16).reshape(experts * blocks, block_rows), before,
        preferred_element_type=jnp.float32,
    ).reshape(experts, blocks, block_rows).astype(jnp.int32)
    rank = jnp.where(hit_blocks, rank, -1)
    number = jnp.arange(slots, dtype=jnp.int32)
    taken = rank[:, :, None, :] == number[None, None, :, None]
    pick = taken.astype(jnp.bfloat16)
    back = (rank[:, :, :, None] == number[None, None, None, :]).astype(jnp.bfloat16)
    slot_weight = jnp.sum(
        jnp.where(taken, weight_blocks[:, :, None, :], 0.0), axis=-1
    ).reshape(experts, blocks * slots, 1)
    total = blocks * slots
    return pl.pallas_call(
        experts_kernel,
        grid=(experts,),
        in_specs=[
            whole(x.shape),
            pl.BlockSpec((1, blocks, slots, block_rows), lambda e: (e, 0, 0, 0)),
            whole(back.shape),
            pl.BlockSpec((1, total, 1), lambda e: (e, 0, 0)),
            pl.BlockSpec((1, D, hidden), lambda e: (e, 0, 0)),
            pl.BlockSpec((1, D, hidden), lambda e: (e, 0, 0)),
            pl.BlockSpec((1, hidden, D), lambda e: (e, 0, 0)),
        ],
        out_specs=whole(x.shape),
        out_shape=jax.ShapeDtypeStruct(x.shape, jnp.bfloat16),
        scratch_shapes=[
            pltpu.VMEM((total, D), jnp.bfloat16),
            pltpu.VMEM((experts, total, D), jnp.bfloat16),
        ],
        compiler_params=pltpu.CompilerParams(vmem_limit_bytes=VMEM_LIMIT),
    )(x, pick, back, slot_weight, w_gate, w_up, w_down)


def exchange(pieces_for, count, index, axis):
    own = pieces_for(index)
    held = jnp.zeros((count,) + own.shape, own.dtype)
    held = lax.dynamic_update_slice_in_dim(held, own[None], index, 0)
    for shift in range(1, count):
        target = lax.rem(index + shift, count)
        source = lax.rem(index + count - shift, count)
        piece = lax.ppermute(
            pieces_for(target), axis, [(i, (i + shift) % count) for i in range(count)]
        )
        held = lax.dynamic_update_slice_in_dim(held, piece[None], source, 0)
    return held


def swap_bit(piece, bit, count):
    return lax.ppermute(piece, "sec", [(i, i ^ (1 << bit)) for i in range(count)])


def halves_reduce(partial, orders, share_rows):
    sec_count = lax.axis_size("sec")
    narrow_count = lax.axis_size("narrow")
    sec_index = lax.axis_index("sec")
    narrow_index = lax.axis_index("narrow")
    bits = sec_count.bit_length() - 1
    wide = partial.shape[1] // len(orders)
    states = []
    for number in range(len(orders)):
        part = partial[:, number * wide : (number + 1) * wide]
        shape = (2,) * bits + (narrow_count, share_rows, wide)
        states.append((part.reshape(shape), list(range(bits - 1, -1, -1)) + ["narrow"]))
    for step in range(bits + 1):
        for number, order in enumerate(orders):
            held, axes = states[number]
            axis = axes.index(order[step])
            if order[step] == "narrow":
                pieces = exchange(
                    lambda peer: lax.dynamic_index_in_dim(held, peer, axis, False),
                    narrow_count, narrow_index, "narrow",
                )
                held = jnp.sum(pieces.astype(jnp.float32), axis=0).astype(jnp.bfloat16)
            else:
                bit = order[step]
                mine = lax.rem(lax.div(sec_index, 1 << bit), 2)
                arrived = swap_bit(
                    lax.dynamic_index_in_dim(held, 1 - mine, axis, False), bit, sec_count
                )
                kept = lax.dynamic_index_in_dim(held, mine, axis, False)
                held = (kept.astype(jnp.float32) + arrived.astype(jnp.float32)).astype(jnp.bfloat16)
            states[number] = (held, axes[:axis] + axes[axis + 1 :])
    return jnp.concatenate([held for held, _ in states], axis=1)


def reduce_orders(sec_count):
    bits = list(range(sec_count.bit_length() - 1))
    first, rest = bits[:1], bits[1:]
    return (
        first + ["narrow"] + rest,
        first + rest + ["narrow"],
    )


def on_device(
    tokens, attn_gain, w_query, w_key, w_value, query_gain, key_gain, w_out, moe_gain,
    expert_ids, expert_weights, w_gate, w_up, w_down,
):
    sec_count = lax.axis_size("sec")
    narrow_count = lax.axis_size("narrow")
    sec_index = lax.axis_index("sec")
    narrow_index = lax.axis_index("narrow")
    local_rows = tokens.shape[0]
    share_rows = local_rows // narrow_count
    expert_here = w_gate.shape[0]
    experts_all = expert_here * sec_count
    capacity = min(share_rows, max(2, 5 * share_rows * TOPK // (2 * experts_all)))
    heads_here = w_query.shape[1] // HEAD
    group_size = HEADS // KV_HEADS
    kv_here = max(1, heads_here // group_size)
    per_key_head = heads_here // kv_here
    part = HEAD // narrow_count
    positions = sec_index * local_rows + jnp.arange(local_rows, dtype=jnp.int32)
    normed = rms_norm(tokens, attn_gain).astype(jnp.bfloat16)

    columns = jnp.arange(w_key.shape[1], dtype=jnp.int32)
    sorted_at = columns % KV_HEADS * part + columns // KV_HEADS
    order = (sorted_at[:, None] == columns[None, :]).astype(jnp.bfloat16)
    both = jnp.concatenate(
        [
            jnp.dot(w, order, preferred_element_type=jnp.float32).astype(jnp.bfloat16)
            for w in (w_key, w_value)
        ],
        axis=1,
    )
    kv_part = jnp.dot(normed, both, preferred_element_type=jnp.float32)
    kv_part = kv_part.reshape(local_rows, 2, KV_HEADS * part)

    def for_peer(peer):
        start = peer * heads_here // group_size * part
        return lax.dynamic_slice_in_dim(kv_part, start, kv_here * part, 2)

    held = exchange(for_peer, narrow_count, narrow_index, "narrow")
    held = held.reshape(narrow_count, local_rows, 2, kv_here, part)
    held = jnp.transpose(held, (1, 2, 3, 0, 4)).reshape(local_rows, 2, kv_here, HEAD)
    keys = rotate(rms_norm(held[:, 0], key_gain), positions).astype(jnp.bfloat16)
    values = held[:, 1].astype(jnp.bfloat16)

    gates_own = expert_weights / jnp.sum(expert_weights, axis=-1, keepdims=True)
    keys_values = jnp.concatenate([keys, values], axis=1).reshape(local_rows, 2 * kv_here * HEAD)
    keys_values = lax.all_gather(keys_values, "sec", axis=0, tiled=True)
    routing = lax.all_gather(
        jnp.concatenate([expert_ids.astype(jnp.float32), gates_own], axis=1), "sec", axis=0,
        tiled=True,
    )
    ids = routing[:, :TOPK].astype(jnp.int32)
    gates = routing[:, TOPK:]

    query = jnp.dot(normed, w_query, preferred_element_type=jnp.float32).reshape(
        local_rows, heads_here, HEAD
    )
    query = rotate(rms_norm(query, query_gain), positions).astype(jnp.bfloat16)
    query = jnp.transpose(query, (1, 0, 2)).reshape(heads_here * local_rows, HEAD)
    attended = attention(query, keys_values, kv_here, per_key_head, local_rows)
    attended = jnp.transpose(
        attended.reshape(heads_here, local_rows, HEAD), (1, 0, 2)
    ).reshape(local_rows, heads_here * HEAD)

    own_offset = narrow_index * share_rows
    mixed = jnp.dot(attended, w_out, preferred_element_type=jnp.float32).astype(jnp.bfloat16)
    mixed = exchange(
        lambda peer: lax.dynamic_slice_in_dim(mixed, peer * share_rows, share_rows, 0),
        narrow_count, narrow_index, "narrow",
    )
    mixed = jnp.sum(mixed.astype(jnp.float32), axis=0)
    tokens_mine = lax.dynamic_slice_in_dim(tokens, own_offset, share_rows, 0)
    carried = (tokens_mine.astype(jnp.float32) + mixed).astype(jnp.bfloat16)
    moe_in = rms_norm(carried, moe_gain).astype(jnp.bfloat16)
    moe_all = lax.all_gather(moe_in, ("sec", "narrow"), axis=0, tiled=True)

    block_rows, slots = local_rows, narrow_count * capacity
    while slots % 16:
        block_rows, slots = 2 * block_rows, 2 * slots
    mixture = experts_local(
        moe_all, ids, gates, (block_rows, slots), w_gate, w_up, w_down, sec_index * expert_here
    )
    mixture = halves_reduce(mixture, reduce_orders(sec_count), share_rows)
    return (carried.astype(jnp.float32) + mixture.astype(jnp.float32)).astype(jnp.bfloat16)


def solution(mesh):
    in_specs = (
        P("sec", None),
        P(),
        P(None, "narrow"),
        P(None, "narrow"),
        P(None, "narrow"),
        P(),
        P(),
        P("narrow", None),
        P(),
        P("sec", None),
        P("sec", None),
        P("sec", None, "narrow"),
        P("sec", None, "narrow"),
        P("sec", "narrow", None),
    )
    out_specs = P(("sec", "narrow"), None)
    return jax.shard_map(
        on_device, mesh=mesh, in_specs=in_specs, out_specs=out_specs, check_vma=False
    )
```
